512 devices in a mesh: agg: 32 (over x, y_hi, core), sub: 16 (over z, y_lo).
Axes of the slice: x: 4, y: 8 (y_hi: 4, y_lo: 2; y = y_hi * 2 + y_lo), z: 8, core: 2. Of those that a mesh axis runs over, the one named last changes fastest.
Arguments:
- stiffness: float32 [1024, 384, 384], P(('agg', 'sub')), as said below
- face_weight: float32 [1024, 384], P(('agg', 'sub')), may hold values from 0.5 to 4
- face_perm: int32 [1024, 384], P(('agg', 'sub')), may hold values from 0 to 383, each once within a row
- agg_size: int32 [1024], P(('agg', 'sub')), may hold values from 192 to 384
- vec_count: int32 [1024], P(('agg', 'sub')), may hold values from 32 to 64
- start_vecs: float32 [1024, 64, 384], P(('agg', 'sub')), may hold values from -6 to 6
- coarse_map: int32 [1024, 64], P(('agg', 'sub')), may hold values from 0 to 511
- coarse_start: float32 [32, 512, 64], P('agg', 'sub'), may hold values from -6 to 6
Outputs:
- fine_basis: float32 [1024, 64, 384], P(('agg', 'sub'))
- coarse_basis: float32 [32, 512, 64], P('agg', 'sub')
The draws below stay inside these ranges and needn't reach their ends.
Inputs may be any that keep to these rules, and one draw needn't show every extreme that they name: Each stiffness block is symmetric with a positive diagonal that exceeds the sum of the absolute values of its row's other entries. Each row of face_perm is a permutation of 0 to 383.
All inputs are finite; a program needn't handle non-finite values.
Results may differ from the reference program's by a relative error of at most 0.0003.
Values sent between devices are 32-bit elements; how exact they have to be, the bound alone decides.
A program may use at most 192 MiB of HBM per device.

```python
import math
import jax
import jax.numpy as jnp
from jax import lax

M = 384
KMAX = 64
KC = 512
KC2 = 64
AGG_DEV = 2
FSTEPS = 8
CSTEPS = 8
AGG_TOTAL = 1024
N_AGG = 32
N_SUB = 16


def draw_stiffness(key, part):

    def one_block(sub_key):
        first_key, second_key = jax.random.split(sub_key)
        raw = jax.random.normal(first_key, (M, M), jnp.float32)
        symmetric = (raw + raw.T) * (0.5 / math.sqrt(M))
        off_diagonal = symmetric * (1.0 - jnp.eye(M, dtype=jnp.float32))
        margin = jnp.exp(jax.random.uniform(second_key, (M,), jnp.float32, math.log(0.1), math.log(2.0)))
        return off_diagonal + jnp.diag(jnp.sum(jnp.abs(off_diagonal), axis=1) + margin)
    block_keys = jax.random.split(jax.random.fold_in(key, 11), AGG_TOTAL)
    return lax.map(one_block, block_keys)


def with_ends(values, stream_key, least, largest):
    longest = values.shape.index(max(values.shape))
    spots = []
    for shift in (0, 1):
        where = [jax.random.randint(jax.random.fold_in(stream_key, axis), (), 0, length) for axis, length in enumerate(values.shape)]
        where[longest] = (where[longest] + shift) % values.shape[longest]
        spots.append(tuple(where))
    return values.at[spots[0]].set(least).at[spots[1]].set(largest)


def levels(stream_key, extent, cuts, low, largest):
    level, own = 1.0, jax.random.fold_in(stream_key, 6)
    for position, shards_of in cuts:
        steps = jnp.exp(jax.random.uniform(jax.random.fold_in(own, position), (shards_of,), jnp.float32, low / len(cuts), largest / len(cuts)))
        level = level * jnp.repeat(steps, extent[position] // shards_of).reshape([-1 if axis == position else 1 for axis in range(len(extent))])
    return level


def normal_values(rng, shape, scale, bound, shards=(), held_as=jnp.bfloat16):
    entries = scale * jax.random.normal(rng, shape, jnp.float32)
    if shards:
        entries = entries * levels(rng, shape, shards, -0.22, 0.18)
    return jnp.clip(entries, -bound, bound).astype(held_as)


def setup_inputs(seed: int = 0) -> dict:
    key_list = jax.random.split(jax.random.key(seed), 9)
    return {
        "stiffness": draw_stiffness(jax.random.fold_in(key_list[8], 71), 0),
        "face_weight": jnp.clip(jnp.exp(math.log(4.0) - 2.0794415 * jax.random.uniform(key_list[1], (AGG_TOTAL, M), jnp.float32) ** levels(key_list[1], (AGG_TOTAL, M), ((0, 512),), -0.2, 0.2)), 0.5, 4.0),
        "face_perm": jax.vmap(lambda own: jax.random.permutation(own, M))(jax.random.split(key_list[2], AGG_TOTAL)).reshape((AGG_TOTAL, M)).astype(jnp.int32),
        "agg_size": with_ends(jax.random.randint(key_list[3], (AGG_TOTAL,), M // 2, M + 1), jax.random.fold_in(key_list[3], 1), M // 2, M).astype(jnp.int32),
        "vec_count": with_ends(jax.random.randint(key_list[4], (AGG_TOTAL,), KMAX // 2, KMAX + 1), jax.random.fold_in(key_list[4], 1), KMAX // 2, KMAX).astype(jnp.int32),
        "start_vecs": normal_values(key_list[5], (AGG_TOTAL, KMAX, M), 1.0, 6.0, ((0, 512),), jnp.float32),
        "coarse_map": with_ends(jax.random.randint(key_list[6], (AGG_TOTAL, KMAX), 0, KC), jax.random.fold_in(key_list[6], 1), 0, KC - 1).astype(jnp.int32),
        "coarse_start": normal_values(key_list[7], (N_AGG, KC, KC2), 1.0, 6.0, ((0, 32), (1, 16)), jnp.float32),
    }


HIGHEST_PRECISION = lax.Precision.HIGHEST

def fine_level(stiffness, face_weight, neighbour, face_perm, agg_size, vec_count, start_vecs, coarse_map):
    fine_order = stiffness.shape[1]
    vec_width = start_vecs.shape[1]
    face_sum = face_weight + jnp.take_along_axis(neighbour, face_perm, axis=1)
    identity = jnp.eye(fine_order, dtype=stiffness.dtype)
    matrix = stiffness + identity[None] * face_sum[:, None, :]
    diagonal = jnp.diagonal(stiffness, axis1=1, axis2=2) + face_sum
    ratio = lax.optimization_barrier(jnp.max(lax.optimization_barrier(jnp.sum(jnp.abs(matrix), axis=2)) / diagonal, axis=1))
    step_scale = 1.0 / (ratio[:, None] * diagonal)
    rows_active = jnp.arange(fine_order, dtype=jnp.int32)[None, :] < agg_size[:, None]
    cols_active = jnp.arange(vec_width, dtype=jnp.int32)[None, :] < vec_count[:, None]
    active = (cols_active[:, :, None] & rows_active[:, None, :]).astype(stiffness.dtype)
    vectors = start_vecs * active
    for sweep in range(FSTEPS):
        applied = jnp.einsum('ikn,inm->ikm', vectors, matrix, precision=HIGHEST_PRECISION)
        vectors = (vectors - step_scale[:, None, :] * applied) * active
    vectors = vectors / jnp.sqrt(lax.optimization_barrier(jnp.sum(vectors * vectors, axis=2, keepdims=True)) + 1e-06)
    applied = jnp.einsum('ikn,inm->ikm', vectors, matrix, precision=HIGHEST_PRECISION)
    coarse_block = jnp.einsum('ikm,ilm->ikl', vectors, applied, precision=HIGHEST_PRECISION)
    selector = (coarse_map[:, :, None] == jnp.arange(KC, dtype=jnp.int32)[None, None, :]).astype(stiffness.dtype)
    spread_rows = jnp.einsum('ikl,ilc->ikc', coarse_block, selector, precision=HIGHEST_PRECISION)
    flat_select = selector.reshape(-1, KC)
    flat_spread = spread_rows.reshape(-1, KC)
    partial_value = jnp.einsum('kr,kc->rc', flat_select, flat_spread, precision=HIGHEST_PRECISION)
    return (vectors, partial_value)

def coarse_level(partial_value, coarse_start):
    shifted = partial_value + jnp.eye(partial_value.shape[0], dtype=partial_value.dtype)
    diagonal = jnp.diagonal(shifted)
    ratio = jnp.max(lax.optimization_barrier(jnp.sum(jnp.abs(shifted), axis=1)) / diagonal)
    step_scale = 1.0 / (ratio * diagonal)
    iterate = coarse_start
    for sweep in range(CSTEPS):
        iterate = iterate - step_scale[:, None] * jnp.dot(shifted, iterate, precision=HIGHEST_PRECISION)
    return iterate / jnp.sqrt(lax.optimization_barrier(jnp.sum(iterate * iterate, axis=0, keepdims=True)) + 1e-06)

def reference(stiffness, face_weight, face_perm, agg_size, vec_count, start_vecs, coarse_map, coarse_start):

    def by_device(array_in):
        return array_in.reshape((N_AGG, N_SUB, AGG_DEV) + array_in.shape[1:])
    neighbour = jnp.roll(by_device(face_weight), 1, axis=0)
    packed = (by_device(stiffness), by_device(face_weight), neighbour, by_device(face_perm), by_device(agg_size), by_device(vec_count), by_device(start_vecs), by_device(coarse_map))

    def per_group(pieces):
        vectors, partial_value = lax.map(lambda inner: fine_level(*inner), pieces)
        return (vectors, lax.optimization_barrier(jnp.sum(partial_value, axis=0)))
    vectors, assembled = lax.map(per_group, packed)
    fine_basis = vectors.reshape(AGG_TOTAL, KMAX, M)
    coarse_basis = lax.map(lambda inner: coarse_level(inner[0], inner[1]), (assembled, coarse_start))
    return (fine_basis, coarse_basis)
```

```python
import jax
import jax.numpy as jnp
from jax import lax
from jax.experimental import pallas as pl
from jax.experimental.pallas import tpu as pltpu
from jax.sharding import PartitionSpec as P

FSTEPS = 8
CSTEPS = 8
F32 = jnp.float32
BF16 = jnp.bfloat16
LANES = 128
NT = (((1,), (1,)), ((), ()))


def halves(x):
    high = x.astype(BF16)
    low = (x - high.astype(F32)).astype(BF16)
    return high, low


def mm(a, b):
    return jnp.dot(a, b, preferred_element_type=F32)


def mm_nt(a, b):
    return lax.dot_general(a, b, NT, preferred_element_type=F32)


def permuted(face, perm):
    tiles = face.shape[1] // LANES
    out = []
    for t in range(tiles):
        index = perm[:, t * LANES : (t + 1) * LANES]
        low, high = index & (LANES - 1), index >> 7
        total = jnp.zeros(index.shape, F32)
        for s in range(tiles):
            picked = jnp.take_along_axis(face[:, s * LANES : (s + 1) * LANES], low, axis=1)
            total = jnp.where(high == s, picked, total)
        out.append(total)
    return jnp.concatenate(out, axis=1)


def diagonal_parts(load, n):
    eye = lax.broadcasted_iota(jnp.int32, (LANES, LANES), 0) == lax.broadcasted_iota(
        jnp.int32, (LANES, LANES), 1
    )
    diags, sums = [], []
    for c in range(n // LANES):
        total = jnp.zeros((8, LANES), F32)
        for r in range(n // LANES):
            tile = load(r, c)
            if r == c:
                diags.append(jnp.sum(jnp.where(eye, tile, 0.0), axis=0, keepdims=True))
                tile = jnp.where(eye, 0.0, tile)
            yield r, c, tile
            total = total + jnp.sum(jnp.abs(tile).reshape(LANES // 8, 8, LANES), axis=0)
        sums.append(jnp.sum(total, axis=0, keepdims=True))
    yield None, jnp.concatenate(diags, axis=1), jnp.concatenate(sums, axis=1)


def split_matrix(load, store, n):
    for item in diagonal_parts(load, n):
        if item[0] is None:
            return item[1], item[2]
        r, c, tile = item
        high, low = halves(tile)
        store(r, c, high, low)


def product(rows, weights):
    high, low = halves(rows)
    top = jnp.concatenate([high, high], axis=1)
    bottom = jnp.concatenate([low, low], axis=1)
    both = mm(jnp.concatenate([top, bottom], axis=0), weights)
    n = rows.shape[0]
    return both[:n] + both[n:]


def make_kernel(n_agg, n_sub, order, width, kc, kc2):
    n_z = n_sub // 2
    rows_own = kc // n_sub

    def kernel(
        stiff, face_w, perm, asize, vcount, start_vecs, cmap, cstart,
        fine_out, coarse_out,
        s_buf, w_buf, v_buf, face_in, meta_tx, meta_rx, blk_tx, blk_rx,
        sel, spread, assembled, aw, x_all, x_tmp,
        load_sem, out_sem, face_sem, meta_send, meta_recv, blk_send, blk_recv,
    ):
        agg, sub = lax.axis_index("agg"), lax.axis_index("sub")
        nxt, prv = lax.rem(agg + 1, n_agg), lax.rem(agg + n_agg - 1, n_agg)
        z, y = sub // 2, lax.rem(sub, 2)

        def peer(r):
            return lax.rem(z + r // 2, n_z) * 2 + lax.rem(y + r % 2, 2)

        def source(r):
            return lax.rem(z + n_z - r // 2, n_z) * 2 + lax.rem(y + r % 2, 2)

        barrier = pltpu.get_barrier_semaphore()
        for other in (nxt, prv):
            pl.semaphore_signal(barrier, inc=1, device_id={"agg": other})
        for r in range(1, n_sub):
            pl.semaphore_signal(barrier, inc=1, device_id={"sub": peer(r)})

        loads = [pltpu.make_async_copy(stiff.at[i], s_buf.at[i], load_sem.at[i]) for i in range(2)]
        loads.append(pltpu.make_async_copy(start_vecs, v_buf, load_sem.at[2]))
        for load in loads:
            load.start()

        own = cstart[0]
        maps = cmap[...].astype(F32)
        meta_tx[0 : rows_own // 2, 0:kc2] = own[: rows_own // 2]
        meta_tx[0 : rows_own // 2, kc2 : 2 * kc2] = own[rows_own // 2 :]
        meta_tx[rows_own // 2 :, :] = jnp.broadcast_to(
            jnp.concatenate([maps[0:1], maps[1:2]], axis=1), (8, LANES)
        )

        pl.semaphore_wait(barrier, n_sub + 1)

        face_copy = pltpu.make_async_remote_copy(
            face_w, face_in, face_sem.at[0], face_sem.at[1], device_id={"agg": nxt}
        )
        face_copy.start()
        metas = []
        for r in range(1, n_sub):
            metas.append(
                pltpu.make_async_remote_copy(
                    meta_tx, meta_rx.at[r], meta_send.at[r], meta_recv.at[r], device_id={"sub": peer(r)}
                )
            )
            metas[-1].start()

        parts = []
        for i in range(2):
            loads[i].wait()

            def load_tile(r, c, i=i):
                return s_buf[i, r * LANES : (r + 1) * LANES, c * LANES : (c + 1) * LANES]

            def store_tile(r, c, high, low, i=i):
                w_buf[i, r * LANES : (r + 1) * LANES, c * LANES : (c + 1) * LANES] = high
                w_buf[i, order + r * LANES : order + (r + 1) * LANES, c * LANES : (c + 1) * LANES] = low

            parts.append(split_matrix(load_tile, store_tile, order))

        loads[2].wait()
        face_copy.wait()
        faces = face_w[...] + permuted(face_in[...], perm[...])

        lane = lax.broadcasted_iota(jnp.int32, (1, order), 1)
        row = lax.broadcasted_iota(jnp.int32, (width, 1), 0)
        vecs, scales, keeps, diags = [], [], [], []
        for i in range(2):
            diag = parts[i][0] + faces[i : i + 1]
            ratio = jnp.max((parts[i][1] + diag) / diag, axis=1, keepdims=True)
            live = lane < asize[i]
            vecs.append(jnp.where((row < vcount[i]) & live, v_buf[i], 0.0))
            scales.append(jnp.where(live, 1.0 / (ratio * diag), 0.0))
            keeps.append(1.0 - 1.0 / ratio)
            diags.append(diag)
        for _ in range(FSTEPS):
            for i in range(2):
                vecs[i] = vecs[i] * keeps[i] - scales[i] * product(vecs[i], w_buf[i])
        mixed = []
        for i in range(2):
            applied = product(vecs[i], w_buf[i]) + vecs[i] * diags[i]
            inverse = 1.0 / jnp.sqrt(jnp.sum(vecs[i] * vecs[i], axis=1, keepdims=True) + 1e-06)
            basis = vecs[i] * inverse
            v_buf[i] = basis
            ah, al = halves(applied * inverse)
            bh, bl = halves(basis)
            quads = mm_nt(jnp.concatenate([ah, al], axis=0), jnp.concatenate([bh, bl], axis=0))
            pair = quads[:width] + quads[width:]
            mixed.append(pair + pltpu.roll(pair, width, 1))
        left = lax.broadcasted_iota(jnp.int32, (width, LANES), 1) < width
        blk_tx[...] = jnp.where(left, mixed[0], mixed[1])
        fine_copy = pltpu.make_async_copy(v_buf, fine_out, out_sem)
        fine_copy.start()

        blocks = []
        for r in range(1, n_sub):
            blocks.append(
                pltpu.make_async_remote_copy(
                    blk_tx, blk_rx.at[r], blk_send.at[r], blk_recv.at[r], device_id={"sub": peer(r)}
                )
            )
            blocks[-1].start()

        coarse_row = lax.broadcasted_iota(jnp.int32, (kc, LANES), 0).astype(F32)
        for r in range(n_sub):
            if r:
                metas[r - 1].wait()
            got = meta_rx[r] if r else meta_tx[...]
            at = pl.multiple_of(source(r) * rows_own, rows_own)
            x_all[pl.ds(at, rows_own // 2), :] = got[: rows_own // 2]
            x_all[pl.ds(at + rows_own // 2, rows_own // 2), :] = pltpu.roll(
                got[: rows_own // 2], kc2, 1
            )
            sel[:, r * LANES : (r + 1) * LANES] = jnp.where(
                coarse_row == got[rows_own // 2 : rows_own // 2 + 1], 1.0, 0.0
            ).astype(BF16)
        x = x_all[:, 0:kc2].T

        batches = [range(0, 4), range(4, 8), range(8, 12), range(12, 16)]
        for b, batch in enumerate(batches):
            for r in batch:
                if r:
                    blocks[r - 1].wait()
                got = blk_rx[r] if r else blk_tx[...]
                square = jnp.concatenate(
                    [jnp.where(left, got, 0.0), jnp.where(left, 0.0, got)], axis=0
                )
                high, low = halves(square)
                one = sel[:, r * LANES : (r + 1) * LANES]
                wide = mm(one, jnp.concatenate([high, low], axis=1))
                high, low = halves(wide[:, :LANES] + wide[:, LANES:])
                spread[0, :, r * LANES : (r + 1) * LANES] = high
                spread[1, :, r * LANES : (r + 1) * LANES] = low
            span = slice(batch[0] * LANES, (batch[-1] + 1) * LANES)
            gain = mm_nt(spread[0, :, span], sel[:, span]) + mm_nt(spread[1, :, span], sel[:, span])
            assembled[...] = gain if b == 0 else assembled[...] + gain

        def load_tile(r, c):
            return assembled[r * LANES : (r + 1) * LANES, c * LANES : (c + 1) * LANES]

        def store_tile(r, c, high, low):
            aw[r * LANES : (r + 1) * LANES, c * LANES : (c + 1) * LANES] = high
            aw[kc + r * LANES : kc + (r + 1) * LANES, c * LANES : (c + 1) * LANES] = low

        cdiag, csum = split_matrix(load_tile, store_tile, kc)
        cdiag = cdiag + 1.0
        ratio = jnp.max((csum + jnp.abs(cdiag)) / cdiag, axis=1, keepdims=True)
        scale = 1.0 / (ratio * cdiag)
        keep = 1.0 - 1.0 / ratio
        for _ in range(CSTEPS):
            x = x * keep - scale * product(x, aw[...])
        x = x / jnp.sqrt(jnp.sum(x * x, axis=1, keepdims=True) + 1e-06)
        for t in range(kc // LANES):
            x_tmp[t] = x[:, t * LANES : (t + 1) * LANES]
        per = LANES // rows_own
        x_all[0:LANES, 0:kc2] = x_tmp[sub // per].T
        coarse_out[0] = x_all[pl.ds(pl.multiple_of(lax.rem(sub, per) * rows_own, rows_own), rows_own), 0:kc2]

        fine_copy.wait()

    return kernel


def local(stiffness, face_weight, face_perm, agg_size, vec_count, start_vecs, coarse_map, coarse_start, n_agg, n_sub):
    order, width = stiffness.shape[1], start_vecs.shape[1]
    rows_own, kc2 = coarse_start.shape[1:]
    kc = rows_own * n_sub
    vmem = pl.BlockSpec(memory_space=pltpu.VMEM)
    smem = pl.BlockSpec(memory_space=pltpu.SMEM)
    hbm = pl.BlockSpec(memory_space=pl.ANY)
    dma = pltpu.SemaphoreType.DMA
    return pl.pallas_call(
        make_kernel(n_agg, n_sub, order, width, kc, kc2),
        out_shape=(
            jax.ShapeDtypeStruct(start_vecs.shape, F32),
            jax.ShapeDtypeStruct(coarse_start.shape, F32),
        ),
        in_specs=[hbm, vmem, vmem, smem, smem, hbm, vmem, vmem],
        out_specs=(hbm, vmem),
        scratch_shapes=[
            pltpu.VMEM((2, order, order), F32),
            pltpu.VMEM((2, 2 * order, order), BF16),
            pltpu.VMEM((2, width, order), F32),
            pltpu.VMEM((2, order), F32),
            pltpu.VMEM((rows_own // 2 + 8, LANES), F32),
            pltpu.VMEM((n_sub, rows_own // 2 + 8, LANES), F32),
            pltpu.VMEM((width, LANES), F32),
            pltpu.VMEM((n_sub, width, LANES), F32),
            pltpu.VMEM((kc, n_sub * LANES), BF16),
            pltpu.VMEM((2, kc, n_sub * LANES), BF16),
            pltpu.VMEM((kc, kc), F32),
            pltpu.VMEM((2 * kc, kc), BF16),
            pltpu.VMEM((kc, LANES), F32),
            pltpu.VMEM((kc // LANES, kc2, LANES), F32),
            dma((3,)), dma, dma((2,)), dma((n_sub,)), dma((n_sub,)), dma((n_sub,)), dma((n_sub,)),
        ],
        compiler_params=pltpu.CompilerParams(
            collective_id=0, has_side_effects=True, vmem_limit_bytes=40 * 1024 * 1024
        ),
    )(stiffness, face_weight, face_perm, agg_size, vec_count, start_vecs, coarse_map, coarse_start)


def solution(mesh):
    n_agg, n_sub = mesh.shape["agg"], mesh.shape["sub"]
    placed = (
        P(("agg", "sub"), None, None),
        P(("agg", "sub"), None),
        P(("agg", "sub"), None),
        P(("agg", "sub")),
        P(("agg", "sub")),
        P(("agg", "sub"), None, None),
        P(("agg", "sub"), None),
        P("agg", "sub", None),
    )

    def run(*args):
        return local(*args, n_agg, n_sub)

    return jax.shard_map(
        run,
        mesh=mesh,
        in_specs=placed,
        out_specs=(P(("agg", "sub"), None, None), P("agg", "sub", None)),
        check_vma=False,
    )
```

```python
import jax
import jax.numpy as jnp
from jax import lax
from jax.experimental import pallas as pl
from jax.experimental.pallas import tpu as pltpu
from jax.sharding import PartitionSpec as P

FSTEPS = 8
CSTEPS = 8
BATCHES = ((0,), (1, 2, 14), (3, 15, 4, 12), (5, 13, 6, 10), (7, 11, 8, 9))
F32 = jnp.float32
BF16 = jnp.bfloat16
LANES = 128
NT = (((1,), (1,)), ((), ()))


def halves(x):
    high = x.astype(BF16)
    low = (x - high.astype(F32)).astype(BF16)
    return high, low


def mm(a, b):
    return jnp.dot(a, b, preferred_element_type=F32)


def mm_nt(a, b):
    return lax.dot_general(a, b, NT, preferred_element_type=F32)


def permuted(face, perm):
    tiles = face.shape[1] // LANES
    out = []
    for t in range(tiles):
        index = perm[:, t * LANES : (t + 1) * LANES]
        low, high = index & (LANES - 1), index >> 7
        total = jnp.zeros(index.shape, F32)
        for s in range(tiles):
            picked = jnp.take_along_axis(face[:, s * LANES : (s + 1) * LANES], low, axis=1)
            total = jnp.where(high == s, picked, total)
        out.append(total)
    return jnp.concatenate(out, axis=1)


def diagonal_parts(load, n):
    eye = lax.broadcasted_iota(jnp.int32, (LANES, LANES), 0) == lax.broadcasted_iota(
        jnp.int32, (LANES, LANES), 1
    )
    diags, sums = [], []
    for c in range(n // LANES):
        total = jnp.zeros((8, LANES), F32)
        for r in range(n // LANES):
            tile = load(r, c)
            if r == c:
                diags.append(jnp.sum(jnp.where(eye, tile, 0.0), axis=0, keepdims=True))
                tile = jnp.where(eye, 0.0, tile)
            yield r, c, tile
            total = total + jnp.sum(jnp.abs(tile).reshape(LANES // 8, 8, LANES), axis=0)
        sums.append(jnp.sum(total, axis=0, keepdims=True))
    yield None, jnp.concatenate(diags, axis=1), jnp.concatenate(sums, axis=1)


def split_matrix(load, store, n):
    for item in diagonal_parts(load, n):
        if item[0] is None:
            return item[1], item[2]
        r, c, tile = item
        high, low = halves(tile)
        store(r, c, high, low)


def product(rows, weights):
    high, low = halves(rows)
    top = jnp.concatenate([high, high], axis=1)
    bottom = jnp.concatenate([low, low], axis=1)
    both = mm(jnp.concatenate([top, bottom], axis=0), weights)
    n = rows.shape[0]
    return both[:n] + both[n:]


def make_kernel(n_agg, n_sub, order, width, kc, kc2):
    n_z = n_sub // 2
    order_r = sorted(range(1, n_sub), key=lambda r: (min(r // 2, n_z - r // 2), (r % 2)))
    rows_own = kc // n_sub

    def kernel(
        stiff, face_hbm, perm_hbm, asize_hbm, vcount_hbm, start_vecs, cmap_hbm, cstart_hbm,
        v_buf, assembled, x_out,
        face_w, perm, asize, vcount, cmap, cstart,
        s_buf, w_buf, face_in, meta_tx, meta_rx, blk_tx, blk_rx,
        sel, spread, picked, x_all,
        load_sem, face_sem, meta_send, meta_recv, blk_send, blk_recv,
    ):
        agg, sub = lax.axis_index("agg"), lax.axis_index("sub")
        nxt, prv = lax.rem(agg + 1, n_agg), lax.rem(agg + n_agg - 1, n_agg)
        z, y = sub // 2, lax.rem(sub, 2)

        def peer(r):
            return lax.rem(z + r // 2, n_z) * 2 + lax.rem(y + r % 2, 2)

        def source(r):
            return lax.rem(z + n_z - r // 2, n_z) * 2 + lax.rem(y + r % 2, 2)

        barrier = pltpu.get_barrier_semaphore()
        for other in (nxt, prv):
            pl.semaphore_signal(barrier, inc=1, device_id={"agg": other})
        for r in order_r:
            pl.semaphore_signal(barrier, inc=1, device_id={"sub": peer(r)})

        def to_everyone(mine, slots, send_sem, recv_sem):
            copies = {}
            for r in order_r:
                copies[r] = pltpu.make_async_remote_copy(
                    mine, slots.at[r], send_sem.at[r], recv_sem.at[r], device_id={"sub": peer(r)}
                )
                copies[r].start()
            return copies

        pairs = [
            (face_hbm, face_w), (cstart_hbm, cstart), (cmap_hbm, cmap),
            (stiff.at[0], s_buf.at[0]), (stiff.at[1], s_buf.at[1]), (perm_hbm, perm),
            (asize_hbm, asize), (vcount_hbm, vcount), (start_vecs, v_buf),
        ]
        loads = [pltpu.make_async_copy(a, b, load_sem.at[i]) for i, (a, b) in enumerate(pairs)]
        for load in loads:
            load.start()
        for load in loads[:3]:
            load.wait()

        own = cstart[0]
        maps = cmap[...].astype(F32)
        meta_tx[0 : rows_own // 2, 0:kc2] = own[: rows_own // 2]
        meta_tx[0 : rows_own // 2, kc2 : 2 * kc2] = own[rows_own // 2 :]
        meta_tx[rows_own // 2 :, :] = jnp.broadcast_to(
            jnp.concatenate([maps[0:1], maps[1:2]], axis=1), (1, LANES)
        )

        pl.semaphore_wait(barrier, n_sub + 1)

        face_copy = pltpu.make_async_remote_copy(
            face_w, face_in, face_sem.at[0], face_sem.at[1], device_id={"agg": nxt}
        )
        face_copy.start()
        metas = to_everyone(meta_tx, meta_rx, meta_send, meta_recv)

        parts = []
        for i in range(2):
            loads[3 + i].wait()

            def load_tile(r, c, i=i):
                return s_buf[i, r * LANES : (r + 1) * LANES, c * LANES : (c + 1) * LANES]

            def store_tile(r, c, high, low, i=i):
                w_buf[i, r * LANES : (r + 1) * LANES, c * LANES : (c + 1) * LANES] = high
                w_buf[i, order + r * LANES : order + (r + 1) * LANES, c * LANES : (c + 1) * LANES] = low

            parts.append(split_matrix(load_tile, store_tile, order))

        for load in loads[5:]:
            load.wait()
        face_copy.wait()
        faces = face_w[...] + permuted(face_in[...], perm[...])

        lane = lax.broadcasted_iota(jnp.int32, (1, order), 1)
        row = lax.broadcasted_iota(jnp.int32, (width, 1), 0)
        vecs, scales, keeps, diags = [], [], [], []
        for i in range(2):
            diag = parts[i][0] + faces[i : i + 1]
            ratio = jnp.max((parts[i][1] + diag) / diag, axis=1, keepdims=True)
            live = lane < asize[i]
            vecs.append(jnp.where((row < vcount[i]) & live, v_buf[i], 0.0))
            scales.append(jnp.where(live, 1.0 / (ratio * diag), 0.0))
            keeps.append(1.0 - 1.0 / ratio)
            diags.append(diag)
        for sweep in range(FSTEPS):
            for i in range(2):
                vecs[i] = vecs[i] * keeps[i] - scales[i] * product(vecs[i], w_buf[i])
        mixed = []
        for i in range(2):
            applied = product(vecs[i], w_buf[i]) + vecs[i] * diags[i]
            inverse = 1.0 / jnp.sqrt(jnp.sum(vecs[i] * vecs[i], axis=1, keepdims=True) + 1e-06)
            basis = vecs[i] * inverse
            v_buf[i] = basis
            ah, al = halves(applied * inverse)
            bh, bl = halves(basis)
            quads = mm_nt(jnp.concatenate([ah, al], axis=0), jnp.concatenate([bh, bl], axis=0))
            pair = quads[:width] + quads[width:]
            mixed.append(pair + pltpu.roll(pair, width, 1))
        half = width // 2
        k = lax.broadcasted_iota(jnp.int32, (half, LANES), 0)
        lane = lax.broadcasted_iota(jnp.int32, (half, LANES), 1)
        left = lane < width
        column = jnp.where(left, lane, lane - width)
        k = jnp.where(left, k, k + half)
        first, second = [jnp.where(left, m[:half], m[half:]) for m in mixed]
        blk_tx[0:half, :] = jnp.where(column >= k, first, second)
        ends = jnp.sum(jnp.where(column == k, second, 0.0), axis=0, keepdims=True)
        blk_tx[half : half + 1, :] = jnp.where(lane[0:1] < width + half, pltpu.roll(ends, width, 1), ends)
        blocks = to_everyone(blk_tx, blk_rx, blk_send, blk_recv)

        coarse_row = lax.broadcasted_iota(jnp.int32, (kc, LANES), 0).astype(F32)
        for r in range(n_sub):
            if r:
                metas[r].wait()
            got = meta_rx[r] if r else meta_tx[...]
            at = pl.multiple_of(source(r) * rows_own, rows_own)
            x_all[pl.ds(at, rows_own // 2), :] = got[: rows_own // 2]
            x_all[pl.ds(at + rows_own // 2, rows_own // 2), :] = pltpu.roll(
                got[: rows_own // 2], kc2, 1
            )
            sel[:, r * LANES : (r + 1) * LANES] = jnp.where(
                coarse_row == got[rows_own // 2 : rows_own // 2 + 1], 1.0, 0.0
            ).astype(BF16)
        x_out[...] = x_all[:, 0:kc2].T

        rows = lax.broadcasted_iota(jnp.int32, (LANES, LANES), 0)
        cols = lax.broadcasted_iota(jnp.int32, (LANES, LANES), 1)
        top, early = rows < width, cols < width
        as_is = (top & early & (rows <= cols)) | (~top & ~early & (rows > cols))
        turned = (top & early & (rows > cols)) | (~top & ~early & (rows < cols))
        ends_at = ~top & (rows == cols)

        def assemble(batch, slot, begin):
            for n, r in enumerate(batch):
                got = blk_rx[r] if r else blk_tx[...]
                own, rolled = got[:half], pltpu.roll(got[:half], width, 1)
                upper, lower = jnp.where(left, own, rolled), jnp.where(left, rolled, own)
                whole = jnp.concatenate([upper, lower, upper, lower], axis=0)
                square = jnp.where(as_is, whole, jnp.where(turned, whole.T, 0.0))
                square = jnp.where(ends_at, got[half : half + 1], square)
                high, low = halves(square)
                one = sel[:, r * LANES : (r + 1) * LANES]
                wide = mm(one, jnp.concatenate([high, low], axis=1))
                high, low = halves(wide[:, :LANES] + wide[:, LANES:])
                at = (slot + n) * LANES
                spread[:, at : at + LANES] = high
                spread[:, n_sub * LANES + at : n_sub * LANES + at + LANES] = low
                picked[:, at : at + LANES] = one
            at, to = slot * LANES, (slot + len(batch)) * LANES
            past = n_sub * LANES
            gain = mm_nt(spread[:, at:to], picked[:, at:to]) + mm_nt(
                spread[:, past + at : past + to], picked[:, at:to]
            )
            assembled[...] = gain if begin else assembled[...] + gain

        slot = 0
        for batch in BATCHES:
            for r in batch:
                if r:
                    blocks[r].wait()
            assemble(batch, slot, slot == 0)
            slot += len(batch)

    return kernel


def make_coarse(n_sub, kc, kc2):
    rows_own = kc // n_sub

    def kernel(basis, assembled, x_in, fine_out, coarse_out, aw, x_tmp, x_cols, x_own, out_sem):
        sub = lax.axis_index("sub")
        copies = [pltpu.make_async_copy(basis, fine_out, out_sem.at[0])]
        copies[0].start()

        def load_tile(r, c):
            return assembled[r * LANES : (r + 1) * LANES, c * LANES : (c + 1) * LANES]

        def store_tile(r, c, high, low):
            aw[r * LANES : (r + 1) * LANES, c * LANES : (c + 1) * LANES] = high
            aw[kc + r * LANES : kc + (r + 1) * LANES, c * LANES : (c + 1) * LANES] = low

        cdiag, csum = split_matrix(load_tile, store_tile, kc)
        cdiag = cdiag + 1.0
        ratio = jnp.max((csum + jnp.abs(cdiag)) / cdiag, axis=1, keepdims=True)
        scale = 1.0 / (ratio * cdiag)
        keep = 1.0 - 1.0 / ratio
        x = x_in[...]
        for _ in range(CSTEPS):
            x = x * keep - scale * product(x, aw[...])
        x = x / jnp.sqrt(jnp.sum(x * x, axis=1, keepdims=True) + 1e-06)
        for t in range(kc // LANES):
            x_tmp[t] = x[:, t * LANES : (t + 1) * LANES]
        per = LANES // rows_own
        x_cols[...] = x_tmp[sub // per].T
        x_own[0] = x_cols[pl.ds(pl.multiple_of(lax.rem(sub, per) * rows_own, rows_own), rows_own), :]
        copies.append(pltpu.make_async_copy(x_own, coarse_out, out_sem.at[1]))
        copies[1].start()

        for copy in copies:
            copy.wait()

    return kernel


def local(stiffness, face_weight, face_perm, agg_size, vec_count, start_vecs, coarse_map, coarse_start, n_agg, n_sub):
    args = (stiffness, face_weight, face_perm, agg_size, vec_count, start_vecs, coarse_map, coarse_start)
    order, width = stiffness.shape[1], start_vecs.shape[1]
    rows_own, kc2 = coarse_start.shape[1:]
    kc = rows_own * n_sub
    vmem = pl.BlockSpec(memory_space=pltpu.VMEM)
    hbm = pl.BlockSpec(memory_space=pltpu.HBM)
    dma = pltpu.SemaphoreType.DMA
    basis, assembled, x = pl.pallas_call(
        make_kernel(n_agg, n_sub, order, width, kc, kc2),
        out_shape=(
            jax.ShapeDtypeStruct(start_vecs.shape, F32),
            jax.ShapeDtypeStruct((kc, kc), F32),
            jax.ShapeDtypeStruct((kc2, kc), F32),
        ),
        in_specs=[hbm] * 8,
        out_specs=(vmem, vmem, vmem),
        scratch_shapes=[
            pltpu.VMEM((2, order), F32),
            pltpu.VMEM((2, order), jnp.int32),
            pltpu.SMEM((2,), jnp.int32),
            pltpu.SMEM((2,), jnp.int32),
            pltpu.VMEM((2, width), jnp.int32),
            pltpu.VMEM((1, rows_own, kc2), F32),
            pltpu.VMEM((2, order, order), F32),
            pltpu.VMEM((2, 2 * order, order), BF16),
            pltpu.VMEM((2, order), F32),
            pltpu.VMEM((rows_own // 2 + 1, LANES), F32),
            pltpu.VMEM((n_sub, rows_own // 2 + 1, LANES), F32),
            pltpu.VMEM((width // 2 + 1, LANES), F32),
            pltpu.VMEM((n_sub, width // 2 + 1, LANES), F32),
            pltpu.VMEM((kc, n_sub * LANES), BF16),
            pltpu.VMEM((kc, 2 * n_sub * LANES), BF16),
            pltpu.VMEM((kc, n_sub * LANES), BF16),
            pltpu.VMEM((kc, LANES), F32),
            dma((9,)), dma((2,)), dma((n_sub,)), dma((n_sub,)), dma((n_sub,)), dma((n_sub,)),
        ],
        compiler_params=pltpu.CompilerParams(
            collective_id=0, has_side_effects=True, vmem_limit_bytes=32 * 1024 * 1024
        ),
    )(*[pltpu.with_memory_space_constraint(a, pltpu.HBM) for a in args])
    return pl.pallas_call(
        make_coarse(n_sub, kc, kc2),
        out_shape=(
            jax.ShapeDtypeStruct(start_vecs.shape, F32),
            jax.ShapeDtypeStruct(coarse_start.shape, F32),
        ),
        in_specs=[vmem] * 3,
        out_specs=(hbm, hbm),
        scratch_shapes=[
            pltpu.VMEM((2 * kc, kc), BF16),
            pltpu.VMEM((kc // LANES, kc2, LANES), F32),
            pltpu.VMEM((LANES, kc2), F32),
            pltpu.VMEM((1, rows_own, kc2), F32),
            dma((2,)),
        ],
        compiler_params=pltpu.CompilerParams(vmem_limit_bytes=16 * 1024 * 1024),
    )(basis, assembled, x)


def solution(mesh):
    n_agg, n_sub = mesh.shape["agg"], mesh.shape["sub"]
    placed = (
        P(("agg", "sub"), None, None),
        P(("agg", "sub"), None),
        P(("agg", "sub"), None),
        P(("agg", "sub")),
        P(("agg", "sub")),
        P(("agg", "sub"), None, None),
        P(("agg", "sub"), None),
        P("agg", "sub", None),
    )

    def run(*args):
        return local(*args, n_agg, n_sub)

    return jax.shard_map(
        run,
        mesh=mesh,
        in_specs=placed,
        out_specs=(P(("agg", "sub"), None, None), P("agg", "sub", None)),
        check_vma=False,
    )
```

```python
import jax
import jax.numpy as jnp
from jax import lax
from jax.experimental import pallas as pl
from jax.experimental.pallas import tpu as pltpu
from jax.sharding import PartitionSpec as P

FSTEPS = 8
CSTEPS = 8
BATCHES = ((0,), (1, 2, 14), (3, 15, 4, 12), (5, 13, 6, 10), (7, 11, 8, 9))
F32 = jnp.float32
BF16 = jnp.bfloat16
LANES = 128
NT = (((1,), (1,)), ((), ()))


def halves(x):
    high = x.astype(BF16)
    low = (x - high.astype(F32)).astype(BF16)
    return high, low


def mm(a, b):
    return jnp.dot(a, b, preferred_element_type=F32)


def mm_nt(a, b):
    return lax.dot_general(a, b, NT, preferred_element_type=F32)


def permuted(face, perm):
    tiles = face.shape[1] // LANES
    out = []
    for t in range(tiles):
        index = perm[:, t * LANES : (t + 1) * LANES]
        low, high = index & (LANES - 1), index >> 7
        total = jnp.zeros(index.shape, F32)
        for s in range(tiles):
            picked = jnp.take_along_axis(face[:, s * LANES : (s + 1) * LANES], low, axis=1)
            total = jnp.where(high == s, picked, total)
        out.append(total)
    return jnp.concatenate(out, axis=1)


def diagonal_parts(load, n):
    eye = lax.broadcasted_iota(jnp.int32, (LANES, LANES), 0) == lax.broadcasted_iota(
        jnp.int32, (LANES, LANES), 1
    )
    diags, sums = [], []
    for c in range(n // LANES):
        total = jnp.zeros((8, LANES), F32)
        for r in range(n // LANES):
            tile = load(r, c)
            if r == c:
                diags.append(jnp.sum(jnp.where(eye, tile, 0.0), axis=0, keepdims=True))
                tile = jnp.where(eye, 0.0, tile)
            yield r, c, tile
            total = total + jnp.sum(jnp.abs(tile).reshape(LANES // 8, 8, LANES), axis=0)
        sums.append(jnp.sum(total, axis=0, keepdims=True))
    yield None, jnp.concatenate(diags, axis=1), jnp.concatenate(sums, axis=1)


def split_matrix(load, store, n):
    for item in diagonal_parts(load, n):
        if item[0] is None:
            return item[1], item[2]
        r, c, tile = item
        high, low = halves(tile)
        store(r, c, high, low)


def product(rows, weights):
    high, low = halves(rows)
    top = jnp.concatenate([high, high], axis=1)
    bottom = jnp.concatenate([low, low], axis=1)
    both = mm(jnp.concatenate([top, bottom], axis=0), weights)
    n = rows.shape[0]
    return both[:n] + both[n:]


def product3(rows, weights):
    high, low = halves(rows)
    n, k = rows.shape
    both = mm(jnp.concatenate([high, low], axis=0), weights[:k])
    return both[:n] + both[n:] + mm(high, weights[k:])


def make_kernel(n_agg, n_sub, order, width, kc, kc2):
    n_z = n_sub // 2
    order_r = sorted(range(1, n_sub), key=lambda r: (min(r // 2, n_z - r // 2), (r % 2)))
    rows_own = kc // n_sub

    def kernel(
        stiff, face_hbm, perm_hbm, asize_hbm, vcount_hbm, start_vecs, cmap_hbm, cstart_hbm,
        v_buf, assembled, x_out,
        face_w, perm, asize, vcount, cmap, cstart,
        s_buf, w_buf, face_in, meta_tx, meta_rx, blk_tx, blk_rx,
        sel, spread, picked, x_all,
        load_sem, face_sem, meta_send, meta_recv, blk_send, blk_recv,
    ):
        agg, sub = lax.axis_index("agg"), lax.axis_index("sub")
        nxt, prv = lax.rem(agg + 1, n_agg), lax.rem(agg + n_agg - 1, n_agg)
        z, y = sub // 2, lax.rem(sub, 2)

        def peer(r):
            return lax.rem(z + r // 2, n_z) * 2 + lax.rem(y + r % 2, 2)

        def source(r):
            return lax.rem(z + n_z - r // 2, n_z) * 2 + lax.rem(y + r % 2, 2)

        barrier = pltpu.get_barrier_semaphore()
        for other in (nxt, prv):
            pl.semaphore_signal(barrier, inc=1, device_id={"agg": other})
        for r in order_r:
            pl.semaphore_signal(barrier, inc=1, device_id={"sub": peer(r)})

        def to_everyone(mine, slots, send_sem, recv_sem):
            copies = {}
            for r in order_r:
                copies[r] = pltpu.make_async_remote_copy(
                    mine, slots.at[r], send_sem.at[r], recv_sem.at[r], device_id={"sub": peer(r)}
                )
                copies[r].start()
            return copies

        pairs = [
            (face_hbm, face_w), (cstart_hbm, cstart), (cmap_hbm, cmap),
            (stiff.at[0], s_buf.at[0]), (stiff.at[1], s_buf.at[1]), (perm_hbm, perm),
            (asize_hbm, asize), (vcount_hbm, vcount), (start_vecs, v_buf),
        ]
        loads = [pltpu.make_async_copy(a, b, load_sem.at[i]) for i, (a, b) in enumerate(pairs)]
        for load in loads:
            load.start()
        for load in loads[:3]:
            load.wait()

        own = cstart[0]
        maps = cmap[...].astype(F32)
        meta_tx[0 : rows_own // 2, 0:kc2] = own[: rows_own // 2]
        meta_tx[0 : rows_own // 2, kc2 : 2 * kc2] = own[rows_own // 2 :]
        meta_tx[rows_own // 2 :, :] = jnp.broadcast_to(
            jnp.concatenate([maps[0:1], maps[1:2]], axis=1), (1, LANES)
        )

        pl.semaphore_wait(barrier, n_sub + 1)

        face_copy = pltpu.make_async_remote_copy(
            face_w, face_in, face_sem.at[0], face_sem.at[1], device_id={"agg": nxt}
        )
        face_copy.start()
        metas = to_everyone(meta_tx, meta_rx, meta_send, meta_recv)

        parts = []
        for i in range(2):
            loads[3 + i].wait()

            def load_tile(r, c, i=i):
                return s_buf[i, r * LANES : (r + 1) * LANES, c * LANES : (c + 1) * LANES]

            def store_tile(r, c, high, low, i=i):
                w_buf[i, r * LANES : (r + 1) * LANES, c * LANES : (c + 1) * LANES] = high
                w_buf[i, order + r * LANES : order + (r + 1) * LANES, c * LANES : (c + 1) * LANES] = low

            parts.append(split_matrix(load_tile, store_tile, order))

        for load in loads[5:]:
            load.wait()
        face_copy.wait()
        faces = face_w[...] + permuted(face_in[...], perm[...])

        lane = lax.broadcasted_iota(jnp.int32, (1, order), 1)
        row = lax.broadcasted_iota(jnp.int32, (width, 1), 0)
        vecs, scales, keeps, diags = [], [], [], []
        for i in range(2):
            diag = parts[i][0] + faces[i : i + 1]
            ratio = jnp.max((parts[i][1] + diag) / diag, axis=1, keepdims=True)
            live = lane < asize[i]
            vecs.append(jnp.where((row < vcount[i]) & live, v_buf[i], 0.0))
            scales.append(jnp.where(live, 1.0 / (ratio * diag), 0.0))
            keeps.append(1.0 - 1.0 / ratio)
            diags.append(diag)
        for sweep in range(FSTEPS):
            for i in range(2):
                vecs[i] = vecs[i] * keeps[i] - scales[i] * product(vecs[i], w_buf[i])
        mixed = []
        for i in range(2):
            applied = product(vecs[i], w_buf[i]) + vecs[i] * diags[i]
            inverse = 1.0 / jnp.sqrt(jnp.sum(vecs[i] * vecs[i], axis=1, keepdims=True) + 1e-06)
            basis = vecs[i] * inverse
            v_buf[i] = basis
            ah, al = halves(applied * inverse)
            bh, bl = halves(basis)
            quads = mm_nt(jnp.concatenate([ah, al], axis=0), jnp.concatenate([bh, bl], axis=0))
            pair = quads[:width] + quads[width:]
            mixed.append(pair + pltpu.roll(pair, width, 1))
        half = width // 2
        k = lax.broadcasted_iota(jnp.int32, (half, LANES), 0)
        lane = lax.broadcasted_iota(jnp.int32, (half, LANES), 1)
        left = lane < width
        column = jnp.where(left, lane, lane - width)
        k = jnp.where(left, k, k + half)
        first, second = [jnp.where(left, m[:half], m[half:]) for m in mixed]
        blk_tx[0:half, :] = jnp.where(column >= k, first, second)
        ends = jnp.sum(jnp.where(column == k, second, 0.0), axis=0, keepdims=True)
        blk_tx[half : half + 1, :] = jnp.where(lane[0:1] < width + half, pltpu.roll(ends, width, 1), ends)
        blocks = to_everyone(blk_tx, blk_rx, blk_send, blk_recv)

        coarse_row = lax.broadcasted_iota(jnp.int32, (kc, LANES), 0).astype(F32)
        for r in range(n_sub):
            if r:
                metas[r].wait()
            got = meta_rx[r] if r else meta_tx[...]
            at = pl.multiple_of(source(r) * rows_own, rows_own)
            x_all[pl.ds(at, rows_own // 2), :] = got[: rows_own // 2]
            x_all[pl.ds(at + rows_own // 2, rows_own // 2), :] = pltpu.roll(
                got[: rows_own // 2], kc2, 1
            )
            sel[:, r * LANES : (r + 1) * LANES] = jnp.where(
                coarse_row == got[rows_own // 2 : rows_own // 2 + 1], 1.0, 0.0
            ).astype(BF16)
        x_out[...] = x_all[:, 0:kc2].T

        rows = lax.broadcasted_iota(jnp.int32, (LANES, LANES), 0)
        cols = lax.broadcasted_iota(jnp.int32, (LANES, LANES), 1)
        top, early = rows < width, cols < width
        as_is = (top & early & (rows <= cols)) | (~top & ~early & (rows > cols))
        turned = (top & early & (rows > cols)) | (~top & ~early & (rows < cols))
        ends_at = ~top & (rows == cols)

        def assemble(batch, slot, begin):
            for n, r in enumerate(batch):
                got = blk_rx[r] if r else blk_tx[...]
                own, rolled = got[:half], pltpu.roll(got[:half], width, 1)
                upper, lower = jnp.where(left, own, rolled), jnp.where(left, rolled, own)
                whole = jnp.concatenate([upper, lower, upper, lower], axis=0)
                square = jnp.where(as_is, whole, jnp.where(turned, whole.T, 0.0))
                square = jnp.where(ends_at, got[half : half + 1], square)
                high, low = halves(square)
                one = sel[:, r * LANES : (r + 1) * LANES]
                wide = mm(one, jnp.concatenate([high, low], axis=1))
                high, low = halves(wide[:, :LANES] + wide[:, LANES:])
                at = (slot + n) * LANES
                spread[0:kc, at : at + LANES] = high
                spread[kc : 2 * kc, at : at + LANES] = low
                picked[:, at : at + LANES] = one
            at, to = slot * LANES, (slot + len(batch)) * LANES
            gain = mm_nt(spread[:, at:to], picked[:, at:to])
            gain = gain[:kc] + gain[kc:]
            assembled[...] = gain if begin else assembled[...] + gain

        slot = 0
        for batch in BATCHES:
            for r in batch:
                if r:
                    blocks[r].wait()
            assemble(batch, slot, slot == 0)
            slot += len(batch)

    return kernel


def make_coarse(n_sub, kc, kc2):
    rows_own = kc // n_sub

    def kernel(basis, assembled, x_in, fine_out, coarse_out, aw, x_tmp, x_cols, x_own, out_sem):
        sub = lax.axis_index("sub")
        copies = [pltpu.make_async_copy(basis, fine_out, out_sem.at[0])]
        copies[0].start()

        def load_tile(r, c):
            return assembled[r * LANES : (r + 1) * LANES, c * LANES : (c + 1) * LANES]

        def store_tile(r, c, high, low):
            aw[r * LANES : (r + 1) * LANES, c * LANES : (c + 1) * LANES] = high
            aw[kc + r * LANES : kc + (r + 1) * LANES, c * LANES : (c + 1) * LANES] = low

        cdiag, csum = split_matrix(load_tile, store_tile, kc)
        cdiag = cdiag + 1.0
        ratio = jnp.max((csum + jnp.abs(cdiag)) / cdiag, axis=1, keepdims=True)
        scale = 1.0 / (ratio * cdiag)
        keep = 1.0 - 1.0 / ratio
        x = x_in[...]
        for _ in range(CSTEPS):
            x = x * keep - scale * product3(x, aw)
        x = x / jnp.sqrt(jnp.sum(x * x, axis=1, keepdims=True) + 1e-06)
        for t in range(kc // LANES):
            x_tmp[t] = x[:, t * LANES : (t + 1) * LANES]
        per = LANES // rows_own
        x_cols[...] = x_tmp[sub // per].T
        x_own[0] = x_cols[pl.ds(pl.multiple_of(lax.rem(sub, per) * rows_own, rows_own), rows_own), :]
        copies.append(pltpu.make_async_copy(x_own, coarse_out, out_sem.at[1]))
        copies[1].start()

        for copy in copies:
            copy.wait()

    return kernel


def local(stiffness, face_weight, face_perm, agg_size, vec_count, start_vecs, coarse_map, coarse_start, n_agg, n_sub):
    args = (stiffness, face_weight, face_perm, agg_size, vec_count, start_vecs, coarse_map, coarse_start)
    order, width = stiffness.shape[1], start_vecs.shape[1]
    rows_own, kc2 = coarse_start.shape[1:]
    kc = rows_own * n_sub
    vmem = pl.BlockSpec(memory_space=pltpu.VMEM)
    hbm = pl.BlockSpec(memory_space=pltpu.HBM)
    dma = pltpu.SemaphoreType.DMA
    basis, assembled, x = pl.pallas_call(
        make_kernel(n_agg, n_sub, order, width, kc, kc2),
        out_shape=(
            jax.ShapeDtypeStruct(start_vecs.shape, F32),
            jax.ShapeDtypeStruct((kc, kc), F32),
            jax.ShapeDtypeStruct((kc2, kc), F32),
        ),
        in_specs=[hbm] * 8,
        out_specs=(vmem, vmem, vmem),
        scratch_shapes=[
            pltpu.VMEM((2, order), F32),
            pltpu.VMEM((2, order), jnp.int32),
            pltpu.SMEM((2,), jnp.int32),
            pltpu.SMEM((2,), jnp.int32),
            pltpu.VMEM((2, width), jnp.int32),
            pltpu.VMEM((1, rows_own, kc2), F32),
            pltpu.VMEM((2, order, order), F32),
            pltpu.VMEM((2, 2 * order, order), BF16),
            pltpu.VMEM((2, order), F32),
            pltpu.VMEM((rows_own // 2 + 1, LANES), F32),
            pltpu.VMEM((n_sub, rows_own // 2 + 1, LANES), F32),
            pltpu.VMEM((width // 2 + 1, LANES), F32),
            pltpu.VMEM((n_sub, width // 2 + 1, LANES), F32),
            pltpu.VMEM((kc, n_sub * LANES), BF16),
            pltpu.VMEM((2 * kc, n_sub * LANES), BF16),
            pltpu.VMEM((kc, n_sub * LANES), BF16),
            pltpu.VMEM((kc, LANES), F32),
            dma((9,)), dma((2,)), dma((n_sub,)), dma((n_sub,)), dma((n_sub,)), dma((n_sub,)),
        ],
        compiler_params=pltpu.CompilerParams(
            collective_id=0, has_side_effects=True, vmem_limit_bytes=32 * 1024 * 1024
        ),
    )(*[pltpu.with_memory_space_constraint(a, pltpu.HBM) for a in args])
    return pl.pallas_call(
        make_coarse(n_sub, kc, kc2),
        out_shape=(
            jax.ShapeDtypeStruct(start_vecs.shape, F32),
            jax.ShapeDtypeStruct(coarse_start.shape, F32),
        ),
        in_specs=[vmem] * 3,
        out_specs=(hbm, hbm),
        scratch_shapes=[
            pltpu.VMEM((2 * kc, kc), BF16),
            pltpu.VMEM((kc // LANES, kc2, LANES), F32),
            pltpu.VMEM((LANES, kc2), F32),
            pltpu.VMEM((1, rows_own, kc2), F32),
            dma((2,)),
        ],
        compiler_params=pltpu.CompilerParams(vmem_limit_bytes=16 * 1024 * 1024),
    )(basis, assembled, x)


def solution(mesh):
    n_agg, n_sub = mesh.shape["agg"], mesh.shape["sub"]
    placed = (
        P(("agg", "sub"), None, None),
        P(("agg", "sub"), None),
        P(("agg", "sub"), None),
        P(("agg", "sub")),
        P(("agg", "sub")),
        P(("agg", "sub"), None, None),
        P(("agg", "sub"), None),
        P("agg", "sub", None),
    )

    def run(*args):
        return local(*args, n_agg, n_sub)

    return jax.shard_map(
        run,
        mesh=mesh,
        in_specs=placed,
        out_specs=(P(("agg", "sub"), None, None), P("agg", "sub", None)),
        check_vma=False,
    )
```

```python
import jax
import jax.numpy as jnp
from jax import lax
from jax.experimental import pallas as pl
from jax.experimental.pallas import tpu as pltpu
from jax.sharding import PartitionSpec as P

FSTEPS = 8
CSTEPS = 8
BATCHES = ((0,), (1, 2, 14, 3), (15, 4, 12, 5), (13, 6, 10, 7, 11, 8, 9))
F32 = jnp.float32
BF16 = jnp.bfloat16
LANES = 128
NT = (((1,), (1,)), ((), ()))


def halves(x):
    high = x.astype(BF16)
    low = (x - high.astype(F32)).astype(BF16)
    return high, low


def mm(a, b):
    return jnp.dot(a, b, preferred_element_type=F32)


def mm_nt(a, b):
    return lax.dot_general(a, b, NT, preferred_element_type=F32)


def permuted(face, perm):
    tiles = face.shape[1] // LANES
    out = []
    for t in range(tiles):
        index = perm[:, t * LANES : (t + 1) * LANES]
        low, high = index & (LANES - 1), index >> 7
        total = jnp.zeros(index.shape, F32)
        for s in range(tiles):
            picked = jnp.take_along_axis(face[:, s * LANES : (s + 1) * LANES], low, axis=1)
            total = jnp.where(high == s, picked, total)
        out.append(total)
    return jnp.concatenate(out, axis=1)


def diagonal_parts(load, n):
    eye = lax.broadcasted_iota(jnp.int32, (LANES, LANES), 0) == lax.broadcasted_iota(
        jnp.int32, (LANES, LANES), 1
    )
    diags, sums = [], []
    for c in range(n // LANES):
        total = jnp.zeros((8, LANES), F32)
        for r in range(n // LANES):
            tile = load(r, c)
            if r == c:
                diags.append(jnp.sum(jnp.where(eye, tile, 0.0), axis=0, keepdims=True))
                tile = jnp.where(eye, 0.0, tile)
            yield r, c, tile
            total = total + jnp.sum(jnp.abs(tile).reshape(LANES // 8, 8, LANES), axis=0)
        sums.append(jnp.sum(total, axis=0, keepdims=True))
    yield None, jnp.concatenate(diags, axis=1), jnp.concatenate(sums, axis=1)


def split_matrix(load, store, n):
    for item in diagonal_parts(load, n):
        if item[0] is None:
            return item[1], item[2]
        r, c, tile = item
        high, low = halves(tile)
        store(r, c, high, low)


def product(rows, weights):
    high, low = halves(rows)
    top = jnp.concatenate([high, high], axis=1)
    bottom = jnp.concatenate([low, low], axis=1)
    both = mm(jnp.concatenate([top, bottom], axis=0), weights)
    n = rows.shape[0]
    return both[:n] + both[n:]


def product3(rows, weights):
    high, low = halves(rows)
    n, k = rows.shape
    both = mm(jnp.concatenate([high, low], axis=0), weights[:k])
    return both[:n] + both[n:] + mm(high, weights[k:])


def make_kernel(n_agg, n_sub, order, width, kc, kc2):
    n_z = n_sub // 2
    order_r = sorted(range(1, n_sub), key=lambda r: (min(r // 2, n_z - r // 2), (r % 2)))
    rows_own = kc // n_sub

    def kernel(
        stiff, face_hbm, perm_hbm, asize_hbm, vcount_hbm, start_vecs, cmap_hbm, cstart_hbm,
        v_buf, aw, crow, x_out,
        face_w, perm, asize, vcount, cmap, cstart,
        s_buf, w_buf, face_in, meta_tx, meta_rx, blk_tx, blk_rx,
        sel, spread, picked, x_all, assembled,
        load_sem, face_sem, meta_send, meta_recv, blk_send, blk_recv,
    ):
        agg, sub = lax.axis_index("agg"), lax.axis_index("sub")
        nxt, prv = lax.rem(agg + 1, n_agg), lax.rem(agg + n_agg - 1, n_agg)
        z, y = sub // 2, lax.rem(sub, 2)

        def peer(r):
            return lax.rem(z + r // 2, n_z) * 2 + lax.rem(y + r % 2, 2)

        def source(r):
            return lax.rem(z + n_z - r // 2, n_z) * 2 + lax.rem(y + r % 2, 2)

        barrier = pltpu.get_barrier_semaphore()
        for other in (prv, nxt):
            pl.semaphore_signal(barrier, inc=1, device_id={"agg": other})
        for r in order_r[::-1]:
            pl.semaphore_signal(barrier, inc=1, device_id={"sub": peer(r)})

        def to_everyone(mine, slots, send_sem, recv_sem):
            copies = {}
            for r in order_r:
                copies[r] = pltpu.make_async_remote_copy(
                    mine, slots.at[r], send_sem.at[r], recv_sem.at[r], device_id={"sub": peer(r)}
                )
                copies[r].start()
            return copies

        pairs = [
            (face_hbm, face_w), (cstart_hbm, cstart), (cmap_hbm, cmap),
            (stiff.at[0], s_buf.at[0]), (stiff.at[1], s_buf.at[1]), (perm_hbm, perm),
            (asize_hbm, asize), (vcount_hbm, vcount), (start_vecs, v_buf),
        ]
        loads = [pltpu.make_async_copy(a, b, load_sem.at[i]) for i, (a, b) in enumerate(pairs)]
        for load in loads:
            load.start()
        for load in loads[:3]:
            load.wait()

        own = cstart[0]
        maps = cmap[...].astype(F32)
        meta_tx[0 : rows_own // 2, 0:kc2] = own[: rows_own // 2]
        meta_tx[0 : rows_own // 2, kc2 : 2 * kc2] = own[rows_own // 2 :]
        meta_tx[rows_own // 2 :, :] = jnp.broadcast_to(
            jnp.concatenate([maps[0:1], maps[1:2]], axis=1), (1, LANES)
        )

        pl.semaphore_wait(barrier, n_sub + 1)

        face_copy = pltpu.make_async_remote_copy(
            face_w, face_in, face_sem.at[0], face_sem.at[1], device_id={"agg": nxt}
        )
        face_copy.start()
        metas = to_everyone(meta_tx, meta_rx, meta_send, meta_recv)

        parts = []
        for i in range(2):
            loads[3 + i].wait()

            def load_tile(r, c, i=i):
                return s_buf[i, r * LANES : (r + 1) * LANES, c * LANES : (c + 1) * LANES]

            def store_tile(r, c, high, low, i=i):
                w_buf[i, r * LANES : (r + 1) * LANES, c * LANES : (c + 1) * LANES] = high
                w_buf[i, order + r * LANES : order + (r + 1) * LANES, c * LANES : (c + 1) * LANES] = low

            parts.append(split_matrix(load_tile, store_tile, order))

        for load in loads[5:]:
            load.wait()
        face_copy.wait()
        faces = face_w[...] + permuted(face_in[...], perm[...])

        lane = lax.broadcasted_iota(jnp.int32, (1, order), 1)
        row = lax.broadcasted_iota(jnp.int32, (width, 1), 0)
        vecs, scales, keeps, diags = [], [], [], []
        for i in range(2):
            diag = parts[i][0] + faces[i : i + 1]
            ratio = jnp.max((parts[i][1] + diag) / diag, axis=1, keepdims=True)
            live = lane < asize[i]
            vecs.append(jnp.where((row < vcount[i]) & live, v_buf[i], 0.0))
            scales.append(jnp.where(live, 1.0 / (ratio * diag), 0.0))
            keeps.append(1.0 - 1.0 / ratio)
            diags.append(diag)
        for sweep in range(FSTEPS):
            for i in range(2):
                vecs[i] = vecs[i] * keeps[i] - scales[i] * product(vecs[i], w_buf[i])
        mixed = []
        for i in range(2):
            applied = product(vecs[i], w_buf[i]) + vecs[i] * diags[i]
            inverse = 1.0 / jnp.sqrt(jnp.sum(vecs[i] * vecs[i], axis=1, keepdims=True) + 1e-06)
            basis = vecs[i] * inverse
            v_buf[i] = basis
            ah, al = halves(applied * inverse)
            bh, bl = halves(basis)
            quads = mm_nt(jnp.concatenate([ah, al], axis=0), jnp.concatenate([bh, bl], axis=0))
            pair = quads[:width] + quads[width:]
            mixed.append(pair + pltpu.roll(pair, width, 1))
        half = width // 2
        k = lax.broadcasted_iota(jnp.int32, (half, LANES), 0)
        lane = lax.broadcasted_iota(jnp.int32, (half, LANES), 1)
        left = lane < width
        column = jnp.where(left, lane, lane - width)
        k = jnp.where(left, k, k + half)
        first, second = [jnp.where(left, m[:half], m[half:]) for m in mixed]
        blk_tx[0:half, :] = jnp.where(column >= k, first, second)
        ends = jnp.sum(jnp.where(column == k, second, 0.0), axis=0, keepdims=True)
        blk_tx[half : half + 1, :] = jnp.where(lane[0:1] < width + half, pltpu.roll(ends, width, 1), ends)
        blocks = to_everyone(blk_tx, blk_rx, blk_send, blk_recv)

        coarse_row = lax.broadcasted_iota(jnp.int32, (kc, LANES), 0).astype(F32)
        for r in range(n_sub):
            if r:
                metas[r].wait()
            got = meta_rx[r] if r else meta_tx[...]
            at = pl.multiple_of(source(r) * rows_own, rows_own)
            x_all[pl.ds(at, rows_own // 2), :] = got[: rows_own // 2]
            x_all[pl.ds(at + rows_own // 2, rows_own // 2), :] = pltpu.roll(
                got[: rows_own // 2], kc2, 1
            )
            sel[:, r * LANES : (r + 1) * LANES] = jnp.where(
                coarse_row == got[rows_own // 2 : rows_own // 2 + 1], 1.0, 0.0
            ).astype(BF16)
        x_out[...] = x_all[:, 0:kc2].T

        rows = lax.broadcasted_iota(jnp.int32, (LANES, LANES), 0)
        cols = lax.broadcasted_iota(jnp.int32, (LANES, LANES), 1)
        top, early = rows < width, cols < width
        as_is = (top & early & (rows <= cols)) | (~top & ~early & (rows > cols))
        turned = (top & early & (rows > cols)) | (~top & ~early & (rows < cols))
        ends_at = ~top & (rows == cols)

        def assemble(batch, slot, begin):
            for n, r in enumerate(batch):
                got = blk_rx[r] if r else blk_tx[...]
                own, rolled = got[:half], pltpu.roll(got[:half], width, 1)
                upper, lower = jnp.where(left, own, rolled), jnp.where(left, rolled, own)
                whole = jnp.concatenate([upper, lower, upper, lower], axis=0)
                square = jnp.where(as_is, whole, jnp.where(turned, whole.T, 0.0))
                square = jnp.where(ends_at, got[half : half + 1], square)
                high, low = halves(square)
                one = sel[:, r * LANES : (r + 1) * LANES]
                wide = mm(jnp.concatenate([one, one], axis=1), jnp.concatenate([high, low], axis=0))
                high, low = halves(wide)
                at = (slot + n) * LANES
                spread[0:kc, at : at + LANES] = high
                spread[kc : 2 * kc, at : at + LANES] = low
                picked[:, at : at + LANES] = one
            at, to = slot * LANES, (slot + len(batch)) * LANES
            def gain(cols):
                both = mm_nt(spread[:, at:to], picked[cols, at:to])
                return both[:kc] + both[kc:]

            if slot + len(batch) < n_sub:
                everything = gain(slice(0, kc))
                assembled[...] = everything if begin else assembled[...] + everything
                return
            part, ready = 2 * LANES, {}

            def load_tile(r, c):
                place = c * LANES // part
                if place not in ready:
                    ready[place] = gain(slice(place * part, (place + 1) * part))
                from_row, from_col = r * LANES, c * LANES
                within = from_col - place * part
                return (
                    assembled[from_row : from_row + LANES, from_col : from_col + LANES]
                    + ready[place][from_row : from_row + LANES, within : within + LANES]
                )

            def store_tile(r, c, high, low):
                aw[r * LANES : (r + 1) * LANES, c * LANES : (c + 1) * LANES] = high
                aw[kc + r * LANES : kc + (r + 1) * LANES, c * LANES : (c + 1) * LANES] = low

            cdiag, csum = split_matrix(load_tile, store_tile, kc)
            crow[0:1, :] = cdiag
            crow[1:2, :] = csum

        slot = 0
        for batch in BATCHES:
            for r in batch:
                if r:
                    blocks[r].wait()
            assemble(batch, slot, slot == 0)
            slot += len(batch)

    return kernel


def make_coarse(n_sub, kc, kc2):
    rows_own = kc // n_sub

    def kernel(basis, aw, crow, x_in, fine_out, coarse_out, x_tmp, x_cols, x_own, out_sem):
        sub = lax.axis_index("sub")
        copies = [pltpu.make_async_copy(basis, fine_out, out_sem.at[0])]
        copies[0].start()

        cdiag, csum = crow[0:1, :], crow[1:2, :]
        cdiag = cdiag + 1.0
        ratio = jnp.max((csum + jnp.abs(cdiag)) / cdiag, axis=1, keepdims=True)
        scale = 1.0 / (ratio * cdiag)
        keep = 1.0 - 1.0 / ratio
        x = x_in[...]
        for _ in range(CSTEPS):
            x = x * keep - scale * product3(x, aw)
        x = x / jnp.sqrt(jnp.sum(x * x, axis=1, keepdims=True) + 1e-06)
        for t in range(kc // LANES):
            x_tmp[t] = x[:, t * LANES : (t + 1) * LANES]
        per = LANES // rows_own
        x_cols[...] = x_tmp[sub // per].T
        x_own[0] = x_cols[pl.ds(pl.multiple_of(lax.rem(sub, per) * rows_own, rows_own), rows_own), :]
        copies.append(pltpu.make_async_copy(x_own, coarse_out, out_sem.at[1]))
        copies[1].start()

        for copy in copies:
            copy.wait()

    return kernel


def local(stiffness, face_weight, face_perm, agg_size, vec_count, start_vecs, coarse_map, coarse_start, n_agg, n_sub):
    args = (stiffness, face_weight, face_perm, agg_size, vec_count, start_vecs, coarse_map, coarse_start)
    order, width = stiffness.shape[1], start_vecs.shape[1]
    rows_own, kc2 = coarse_start.shape[1:]
    kc = rows_own * n_sub
    vmem = pl.BlockSpec(memory_space=pltpu.VMEM)
    hbm = pl.BlockSpec(memory_space=pltpu.HBM)
    dma = pltpu.SemaphoreType.DMA
    basis, aw, crow, x = pl.pallas_call(
        make_kernel(n_agg, n_sub, order, width, kc, kc2),
        out_shape=(
            jax.ShapeDtypeStruct(start_vecs.shape, F32),
            jax.ShapeDtypeStruct((2 * kc, kc), BF16),
            jax.ShapeDtypeStruct((8, kc), F32),
            jax.ShapeDtypeStruct((kc2, kc), F32),
        ),
        in_specs=[hbm] * 8,
        out_specs=(vmem,) * 4,
        scratch_shapes=[
            pltpu.VMEM((2, order), F32),
            pltpu.VMEM((2, order), jnp.int32),
            pltpu.SMEM((2,), jnp.int32),
            pltpu.SMEM((2,), jnp.int32),
            pltpu.VMEM((2, width), jnp.int32),
            pltpu.VMEM((1, rows_own, kc2), F32),
            pltpu.VMEM((2, order, order), F32),
            pltpu.VMEM((2, 2 * order, order), BF16),
            pltpu.VMEM((2, order), F32),
            pltpu.VMEM((rows_own // 2 + 1, LANES), F32),
            pltpu.VMEM((n_sub, rows_own // 2 + 1, LANES), F32),
            pltpu.VMEM((width // 2 + 1, LANES), F32),
            pltpu.VMEM((n_sub, width // 2 + 1, LANES), F32),
            pltpu.VMEM((kc, n_sub * LANES), BF16),
            pltpu.VMEM((2 * kc, n_sub * LANES), BF16),
            pltpu.VMEM((kc, n_sub * LANES), BF16),
            pltpu.VMEM((kc, LANES), F32),
            pltpu.VMEM((kc, kc), F32),
            dma((9,)), dma((2,)), dma((n_sub,)), dma((n_sub,)), dma((n_sub,)), dma((n_sub,)),
        ],
        compiler_params=pltpu.CompilerParams(
            collective_id=0, has_side_effects=True, vmem_limit_bytes=32 * 1024 * 1024
        ),
    )(*[pltpu.with_memory_space_constraint(a, pltpu.HBM) for a in args])
    return pl.pallas_call(
        make_coarse(n_sub, kc, kc2),
        out_shape=(
            jax.ShapeDtypeStruct(start_vecs.shape, F32),
            jax.ShapeDtypeStruct(coarse_start.shape, F32),
        ),
        in_specs=[vmem] * 4,
        out_specs=(hbm, hbm),
        scratch_shapes=[
            pltpu.VMEM((kc // LANES, kc2, LANES), F32),
            pltpu.VMEM((LANES, kc2), F32),
            pltpu.VMEM((1, rows_own, kc2), F32),
            dma((2,)),
        ],
        compiler_params=pltpu.CompilerParams(vmem_limit_bytes=16 * 1024 * 1024),
    )(basis, aw, crow, x)


def solution(mesh):
    n_agg, n_sub = mesh.shape["agg"], mesh.shape["sub"]
    placed = (
        P(("agg", "sub"), None, None),
        P(("agg", "sub"), None),
        P(("agg", "sub"), None),
        P(("agg", "sub")),
        P(("agg", "sub")),
        P(("agg", "sub"), None, None),
        P(("agg", "sub"), None),
        P("agg", "sub", None),
    )

    def run(*args):
        return local(*args, n_agg, n_sub)

    return jax.shard_map(
        run,
        mesh=mesh,
        in_specs=placed,
        out_specs=(P(("agg", "sub"), None, None), P("agg", "sub", None)),
        check_vma=False,
    )
```

```python
import jax
import jax.numpy as jnp
from jax import lax
from jax.experimental import pallas as pl
from jax.experimental.pallas import tpu as pltpu
from jax.sharding import PartitionSpec as P

FSTEPS = 8
CSTEPS = 8
BATCHES = ((0,), (1, 2, 14, 3), (15, 4, 12, 5), (13, 6, 10, 7, 11, 8, 9))
F32 = jnp.float32
BF16 = jnp.bfloat16
LANES = 128
NT = (((1,), (1,)), ((), ()))


def halves(x):
    high = x.astype(BF16)
    low = (x - high.astype(F32)).astype(BF16)
    return high, low


def mm(a, b):
    return jnp.dot(a, b, preferred_element_type=F32)


def mm_nt(a, b):
    return lax.dot_general(a, b, NT, preferred_element_type=F32)


def permuted(face, perm):
    tiles = face.shape[1] // LANES
    out = []
    for t in range(tiles):
        index = perm[:, t * LANES : (t + 1) * LANES]
        low, high = index & (LANES - 1), index >> 7
        total = jnp.zeros(index.shape, F32)
        for s in range(tiles):
            picked = jnp.take_along_axis(face[:, s * LANES : (s + 1) * LANES], low, axis=1)
            total = jnp.where(high == s, picked, total)
        out.append(total)
    return jnp.concatenate(out, axis=1)


def diagonal_parts(load, n):
    eye = lax.broadcasted_iota(jnp.int32, (LANES, LANES), 0) == lax.broadcasted_iota(
        jnp.int32, (LANES, LANES), 1
    )
    diags, sums = [], []
    for c in range(n // LANES):
        total = jnp.zeros((8, LANES), F32)
        for r in range(n // LANES):
            tile = load(r, c)
            if r == c:
                diags.append(jnp.sum(jnp.where(eye, tile, 0.0), axis=0, keepdims=True))
                tile = jnp.where(eye, 0.0, tile)
            yield r, c, tile
            total = total + jnp.sum(jnp.abs(tile).reshape(LANES // 8, 8, LANES), axis=0)
        sums.append(jnp.sum(total, axis=0, keepdims=True))
    yield None, jnp.concatenate(diags, axis=1), jnp.concatenate(sums, axis=1)


def split_matrix(load, store, n):
    for item in diagonal_parts(load, n):
        if item[0] is None:
            return item[1], item[2]
        r, c, tile = item
        high, low = halves(tile)
        store(r, c, high, low)


def product(rows, weights):
    high, low = halves(rows)
    top = jnp.concatenate([high, high], axis=1)
    bottom = jnp.concatenate([low, low], axis=1)
    both = mm(jnp.concatenate([top, bottom], axis=0), weights)
    n = rows.shape[0]
    return both[:n] + both[n:]


def product3(rows, weights):
    high, low = halves(rows)
    n, k = rows.shape
    both = mm(jnp.concatenate([high, low], axis=0), weights[:k])
    return both[:n] + both[n:] + mm(high, weights[k:])


def make_kernel(n_agg, n_sub, order, width, kc, kc2):
    n_z = n_sub // 2
    order_r = sorted(range(1, n_sub), key=lambda r: (min(r // 2, n_z - r // 2), (r % 2)))
    rows_own = kc // n_sub

    def kernel(
        stiff, face_hbm, perm_hbm, asize_hbm, vcount_hbm, start_vecs, cmap_hbm, cstart_hbm,
        v_buf, aw, crow, x_out,
        face_w, perm, asize, vcount, cmap, cstart,
        s_buf, w_buf, face_in, meta_tx, meta_rx, blk_tx, blk_rx,
        sel, spread, picked, x_all, assembled,
        load_sem, face_sem, meta_send, meta_recv, blk_send, blk_recv,
    ):
        agg, sub = lax.axis_index("agg"), lax.axis_index("sub")
        nxt, prv = lax.rem(agg + 1, n_agg), lax.rem(agg + n_agg - 1, n_agg)
        z, y = sub // 2, lax.rem(sub, 2)

        def peer(r):
            return lax.rem(z + r // 2, n_z) * 2 + lax.rem(y + r % 2, 2)

        def source(r):
            return lax.rem(z + n_z - r // 2, n_z) * 2 + lax.rem(y + r % 2, 2)

        barrier = pltpu.get_barrier_semaphore()
        for other in (prv, nxt):
            pl.semaphore_signal(barrier, inc=1, device_id={"agg": other})
        for r in order_r[::-1]:
            pl.semaphore_signal(barrier, inc=1, device_id={"sub": peer(r)})

        def to_everyone(mine, slots, send_sem, recv_sem):
            copies = {}
            for r in order_r:
                copies[r] = pltpu.make_async_remote_copy(
                    mine, slots.at[r], send_sem.at[r], recv_sem.at[r], device_id={"sub": peer(r)}
                )
                copies[r].start()
            return copies

        pairs = [
            (face_hbm, face_w), (cstart_hbm, cstart), (cmap_hbm, cmap),
            (stiff.at[0], s_buf.at[0]), (stiff.at[1], s_buf.at[1]), (perm_hbm, perm),
            (asize_hbm, asize), (vcount_hbm, vcount), (start_vecs, v_buf),
        ]
        loads = [pltpu.make_async_copy(a, b, load_sem.at[i]) for i, (a, b) in enumerate(pairs)]
        for load in loads:
            load.start()
        for load in loads[:3]:
            load.wait()

        own = cstart[0]
        maps = cmap[...].astype(F32)
        meta_tx[0 : rows_own // 2, 0:kc2] = own[: rows_own // 2]
        meta_tx[0 : rows_own // 2, kc2 : 2 * kc2] = own[rows_own // 2 :]
        meta_tx[rows_own // 2 :, :] = jnp.broadcast_to(
            jnp.concatenate([maps[0:1], maps[1:2]], axis=1), (1, LANES)
        )

        pl.semaphore_wait(barrier, n_sub + 1)

        face_copy = pltpu.make_async_remote_copy(
            face_w, face_in, face_sem.at[0], face_sem.at[1], device_id={"agg": nxt}
        )
        face_copy.start()
        metas = to_everyone(meta_tx, meta_rx, meta_send, meta_recv)

        parts = []
        for i in range(2):
            loads[3 + i].wait()

            def load_tile(r, c, i=i):
                return s_buf[i, r * LANES : (r + 1) * LANES, c * LANES : (c + 1) * LANES]

            def store_tile(r, c, high, low, i=i):
                w_buf[i, r * LANES : (r + 1) * LANES, c * LANES : (c + 1) * LANES] = high
                w_buf[i, order + r * LANES : order + (r + 1) * LANES, c * LANES : (c + 1) * LANES] = low

            parts.append(split_matrix(load_tile, store_tile, order))

        for load in loads[5:]:
            load.wait()
        face_copy.wait()
        faces = face_w[...] + permuted(face_in[...], perm[...])

        lane = lax.broadcasted_iota(jnp.int32, (1, order), 1)
        row = lax.broadcasted_iota(jnp.int32, (width, 1), 0)
        vecs, scales, keeps, diags = [], [], [], []
        for i in range(2):
            diag = parts[i][0] + faces[i : i + 1]
            ratio = jnp.max((parts[i][1] + diag) / diag, axis=1, keepdims=True)
            live = lane < asize[i]
            vecs.append(jnp.where((row < vcount[i]) & live, v_buf[i], 0.0))
            scales.append(jnp.where(live, 1.0 / (ratio * diag), 0.0))
            keeps.append(1.0 - 1.0 / ratio)
            diags.append(diag)
        for sweep in range(FSTEPS):
            for i in range(2):
                vecs[i] = vecs[i] * keeps[i] - scales[i] * product3(vecs[i], w_buf.at[i])
        mixed = []
        for i in range(2):
            applied = product(vecs[i], w_buf[i]) + vecs[i] * diags[i]
            inverse = 1.0 / jnp.sqrt(jnp.sum(vecs[i] * vecs[i], axis=1, keepdims=True) + 1e-06)
            basis = vecs[i] * inverse
            v_buf[i] = basis
            ah, al = halves(applied * inverse)
            bh, bl = halves(basis)
            quads = mm_nt(jnp.concatenate([ah, al], axis=0), jnp.concatenate([bh, bl], axis=0))
            pair = quads[:width] + quads[width:]
            mixed.append(pair + pltpu.roll(pair, width, 1))
        half = width // 2
        k = lax.broadcasted_iota(jnp.int32, (half, LANES), 0)
        lane = lax.broadcasted_iota(jnp.int32, (half, LANES), 1)
        left = lane < width
        column = jnp.where(left, lane, lane - width)
        k = jnp.where(left, k, k + half)
        first, second = [jnp.where(left, m[:half], m[half:]) for m in mixed]
        blk_tx[0:half, :] = jnp.where(column >= k, first, second)
        ends = jnp.sum(jnp.where(column == k, second, 0.0), axis=0, keepdims=True)
        blk_tx[half : half + 1, :] = jnp.where(lane[0:1] < width + half, pltpu.roll(ends, width, 1), ends)
        blocks = to_everyone(blk_tx, blk_rx, blk_send, blk_recv)

        coarse_row = lax.broadcasted_iota(jnp.int32, (kc, LANES), 0).astype(F32)
        for r in range(n_sub):
            if r:
                metas[r].wait()
            got = meta_rx[r] if r else meta_tx[...]
            at = pl.multiple_of(source(r) * rows_own, rows_own)
            x_all[pl.ds(at, rows_own // 2), :] = got[: rows_own // 2]
            x_all[pl.ds(at + rows_own // 2, rows_own // 2), :] = pltpu.roll(
                got[: rows_own // 2], kc2, 1
            )
            sel[:, r * LANES : (r + 1) * LANES] = jnp.where(
                coarse_row == got[rows_own // 2 : rows_own // 2 + 1], 1.0, 0.0
            ).astype(BF16)
        x_out[...] = x_all[:, 0:kc2].T

        rows = lax.broadcasted_iota(jnp.int32, (LANES, LANES), 0)
        cols = lax.broadcasted_iota(jnp.int32, (LANES, LANES), 1)
        top, early = rows < width, cols < width
        as_is = (top & early & (rows <= cols)) | (~top & ~early & (rows > cols))
        turned = (top & early & (rows > cols)) | (~top & ~early & (rows < cols))
        ends_at = ~top & (rows == cols)

        def assemble(batch, slot, begin):
            for n, r in enumerate(batch):
                got = blk_rx[r] if r else blk_tx[...]
                own, rolled = got[:half], pltpu.roll(got[:half], width, 1)
                upper, lower = jnp.where(left, own, rolled), jnp.where(left, rolled, own)
                whole = jnp.concatenate([upper, lower, upper, lower], axis=0)
                square = jnp.where(as_is, whole, jnp.where(turned, whole.T, 0.0))
                square = jnp.where(ends_at, got[half : half + 1], square)
                high, low = halves(square)
                one = sel[:, r * LANES : (r + 1) * LANES]
                wide = mm(jnp.concatenate([one, one], axis=1), jnp.concatenate([high, low], axis=0))
                high, low = halves(wide)
                at = (slot + n) * LANES
                spread[0:kc, at : at + LANES] = high
                spread[kc : 2 * kc, at : at + LANES] = low
                picked[:, at : at + LANES] = one
            at, to = slot * LANES, (slot + len(batch)) * LANES
            def gain(cols):
                both = mm_nt(spread[:, at:to], picked[cols, at:to])
                return both[:kc] + both[kc:]

            if slot + len(batch) < n_sub:
                everything = gain(slice(0, kc))
                assembled[...] = everything if begin else assembled[...] + everything
                return
            part, ready = 2 * LANES, {}

            def load_tile(r, c):
                place = c * LANES // part
                if place not in ready:
                    ready[place] = gain(slice(place * part, (place + 1) * part))
                from_row, from_col = r * LANES, c * LANES
                within = from_col - place * part
                return (
                    assembled[from_row : from_row + LANES, from_col : from_col + LANES]
                    + ready[place][from_row : from_row + LANES, within : within + LANES]
                )

            def store_tile(r, c, high, low):
                aw[r * LANES : (r + 1) * LANES, c * LANES : (c + 1) * LANES] = high
                aw[kc + r * LANES : kc + (r + 1) * LANES, c * LANES : (c + 1) * LANES] = low

            cdiag, csum = split_matrix(load_tile, store_tile, kc)
            crow[0:1, :] = cdiag
            crow[1:2, :] = csum

        slot = 0
        for batch in BATCHES:
            for r in batch:
                if r:
                    blocks[r].wait()
            assemble(batch, slot, slot == 0)
            slot += len(batch)

    return kernel


def make_coarse(n_sub, kc, kc2):
    rows_own = kc // n_sub

    def kernel(basis, aw, crow, x_in, fine_out, coarse_out, x_tmp, x_cols, x_own, out_sem):
        sub = lax.axis_index("sub")
        copies = [pltpu.make_async_copy(basis, fine_out, out_sem.at[0])]
        copies[0].start()

        cdiag, csum = crow[0:1, :], crow[1:2, :]
        cdiag = cdiag + 1.0
        ratio = jnp.max((csum + jnp.abs(cdiag)) / cdiag, axis=1, keepdims=True)
        scale = 1.0 / (ratio * cdiag)
        keep = 1.0 - 1.0 / ratio
        x = x_in[...]
        for _ in range(CSTEPS):
            x = x * keep - scale * product3(x, aw)
        x = x / jnp.sqrt(jnp.sum(x * x, axis=1, keepdims=True) + 1e-06)
        for t in range(kc // LANES):
            x_tmp[t] = x[:, t * LANES : (t + 1) * LANES]
        per = LANES // rows_own
        x_cols[...] = x_tmp[sub // per].T
        x_own[0] = x_cols[pl.ds(pl.multiple_of(lax.rem(sub, per) * rows_own, rows_own), rows_own), :]
        copies.append(pltpu.make_async_copy(x_own, coarse_out, out_sem.at[1]))
        copies[1].start()

        for copy in copies:
            copy.wait()

    return kernel


def local(stiffness, face_weight, face_perm, agg_size, vec_count, start_vecs, coarse_map, coarse_start, n_agg, n_sub):
    args = (stiffness, face_weight, face_perm, agg_size, vec_count, start_vecs, coarse_map, coarse_start)
    order, width = stiffness.shape[1], start_vecs.shape[1]
    rows_own, kc2 = coarse_start.shape[1:]
    kc = rows_own * n_sub
    vmem = pl.BlockSpec(memory_space=pltpu.VMEM)
    hbm = pl.BlockSpec(memory_space=pltpu.HBM)
    dma = pltpu.SemaphoreType.DMA
    basis, aw, crow, x = pl.pallas_call(
        make_kernel(n_agg, n_sub, order, width, kc, kc2),
        out_shape=(
            jax.ShapeDtypeStruct(start_vecs.shape, F32),
            jax.ShapeDtypeStruct((2 * kc, kc), BF16),
            jax.ShapeDtypeStruct((8, kc), F32),
            jax.ShapeDtypeStruct((kc2, kc), F32),
        ),
        in_specs=[hbm] * 8,
        out_specs=(vmem,) * 4,
        scratch_shapes=[
            pltpu.VMEM((2, order), F32),
            pltpu.VMEM((2, order), jnp.int32),
            pltpu.SMEM((2,), jnp.int32),
            pltpu.SMEM((2,), jnp.int32),
            pltpu.VMEM((2, width), jnp.int32),
            pltpu.VMEM((1, rows_own, kc2), F32),
            pltpu.VMEM((2, order, order), F32),
            pltpu.VMEM((2, 2 * order, order), BF16),
            pltpu.VMEM((2, order), F32),
            pltpu.VMEM((rows_own // 2 + 1, LANES), F32),
            pltpu.VMEM((n_sub, rows_own // 2 + 1, LANES), F32),
            pltpu.VMEM((width // 2 + 1, LANES), F32),
            pltpu.VMEM((n_sub, width // 2 + 1, LANES), F32),
            pltpu.VMEM((kc, n_sub * LANES), BF16),
            pltpu.VMEM((2 * kc, n_sub * LANES), BF16),
            pltpu.VMEM((kc, n_sub * LANES), BF16),
            pltpu.VMEM((kc, LANES), F32),
            pltpu.VMEM((kc, kc), F32),
            dma((9,)), dma((2,)), dma((n_sub,)), dma((n_sub,)), dma((n_sub,)), dma((n_sub,)),
        ],
        compiler_params=pltpu.CompilerParams(
            collective_id=0, has_side_effects=True, vmem_limit_bytes=32 * 1024 * 1024
        ),
    )(*[pltpu.with_memory_space_constraint(a, pltpu.HBM) for a in args])
    return pl.pallas_call(
        make_coarse(n_sub, kc, kc2),
        out_shape=(
            jax.ShapeDtypeStruct(start_vecs.shape, F32),
            jax.ShapeDtypeStruct(coarse_start.shape, F32),
        ),
        in_specs=[vmem] * 4,
        out_specs=(hbm, hbm),
        scratch_shapes=[
            pltpu.VMEM((kc // LANES, kc2, LANES), F32),
            pltpu.VMEM((LANES, kc2), F32),
            pltpu.VMEM((1, rows_own, kc2), F32),
            dma((2,)),
        ],
        compiler_params=pltpu.CompilerParams(vmem_limit_bytes=16 * 1024 * 1024),
    )(basis, aw, crow, x)


def solution(mesh):
    n_agg, n_sub = mesh.shape["agg"], mesh.shape["sub"]
    placed = (
        P(("agg", "sub"), None, None),
        P(("agg", "sub"), None),
        P(("agg", "sub"), None),
        P(("agg", "sub")),
        P(("agg", "sub")),
        P(("agg", "sub"), None, None),
        P(("agg", "sub"), None),
        P("agg", "sub", None),
    )

    def run(*args):
        return local(*args, n_agg, n_sub)

    return jax.shard_map(
        run,
        mesh=mesh,
        in_specs=placed,
        out_specs=(P(("agg", "sub"), None, None), P("agg", "sub", None)),
        check_vma=False,
    )
```
